512 devices in a mesh: vocab: 64 (over x, z), width: 8 (over y, core).
Axes of the slice: x: 4, y: 4, z: 16, core: 2. Of those that a mesh axis runs over, the one named last changes fastest.
Arguments:
- hidden_states: bfloat16 [512, 5120], P('vocab', 'width'), may hold values from -12 to 12
- head_weight: bfloat16 [81920, 5120], P('vocab', 'width'), may hold values from -0.26553307 to 0.26553307
- targets: int32 [512], replicated, may hold values from 0 to 81919
- terminal: int32 [512], replicated, may hold values 0 or 1
- cotangent: float32 [512], replicated, may hold values from -6 to 6
Outputs:
- rewards: float32 [512], replicated
- hidden_grad: bfloat16 [512, 5120], P('vocab', 'width')
- weight_grad: bfloat16 [81920, 5120], P('vocab', 'width')
The draws below stay inside these ranges and needn't reach their ends.
All inputs are finite; a program needn't handle non-finite values.
Results may differ from the reference program's by a relative error of at most 0.0051.
Values may be sent and summed in bfloat16 or wider, within the bound.
No kernel may reach another device: no remote copies, remote signals or barrier semaphores. Data moves between devices by JAX's collectives and lax.ppermute only.
A program may use at most 64 MiB of HBM per device.

```python
import math
import jax
import jax.numpy as jnp
import numpy as np

D = 5120
T_SIZE = 512
VOCAB = 81920


def draw_head_weight(key, part):
    key = jax.random.fold_in(key, 2)
    base = jax.random.truncated_normal(key, -6.0, 6.0, (VOCAB, D), jnp.float32)
    return (3.0 * D ** (-0.5) * base).astype(jnp.bfloat16)


def draw_hidden_states(key, part):
    key = jax.random.fold_in(key, 1)
    base = jax.random.truncated_normal(key, -6.0, 6.0, (T_SIZE, D), jnp.float32)
    return base.astype(jnp.bfloat16)


def set_ends(drawn, own_key, low, largest):
    shape = drawn.shape
    index_at = [jax.random.randint(jax.random.fold_in(own_key, axis), (), 0, shape[axis]) for axis in range(len(shape))]
    drawn = drawn.at[tuple(index_at)].set(low)
    longest = shape.index(max(shape))
    index_at[longest] = (index_at[longest] + 1) % shape[longest]
    return drawn.at[tuple(index_at)].set(largest)


def skewed_wide(key, shape, number_of, lean):
    portions = [min(1 << octave, number_of + 1 - (1 << octave)) * (1 << 20) // math.isqrt((1 << octave) ** lean) + 1 for octave in range((number_of + 1).bit_length()) if 1 << octave <= number_of]
    scale = 1 + sum(portions) // (1 << 30)
    grid = np.cumsum(np.array([max(1, weight // scale) for weight in portions]))
    lot = jax.random.randint(jax.random.fold_in(key, 1), shape, 0, int(grid[len(portions) - 1]))
    start = jnp.left_shift(1, jnp.searchsorted(jnp.asarray(grid, jnp.int32), lot, side="right").astype(jnp.int32))
    grade = start - 1 + jax.random.randint(jax.random.fold_in(key, 4), shape, 0, 1 << 30) % jnp.minimum(start, number_of + 1 - start)
    return jax.random.permutation(jax.random.fold_in(key, 2), number_of)[grade].astype(jnp.int32)


def centred(own_key, shape, spread, bound, kind=jnp.bfloat16):
    values = spread * jax.random.normal(own_key, shape, jnp.float32)
    return jnp.clip(values, min=-bound, max=bound).astype(kind)


def setup_inputs(seed: int = 0) -> dict:
    key_list = jax.random.split(jax.random.key(seed), 6)
    return {
        "hidden_states": draw_hidden_states(jax.random.fold_in(key_list[5], 71), 0),
        "head_weight": draw_head_weight(jax.random.fold_in(key_list[5], 71), 0),
        "targets": set_ends(skewed_wide(key_list[2], (T_SIZE,), VOCAB, 2), jax.random.fold_in(key_list[2], 3), 0, VOCAB - 1).astype(jnp.int32),
        "terminal": set_ends((jax.random.randint(key_list[3], (T_SIZE,), 0, 8) < 1).astype(jnp.int32), jax.random.fold_in(key_list[3], 1), 0, 1),
        "cotangent": centred(key_list[4], (T_SIZE,), 1.0, 6.0, jnp.float32),
    }


discount = 0.99


def reference(hidden_states, head_weight, targets, terminal, cotangent):
    logits = jnp.dot(hidden_states, head_weight.T, preferred_element_type=jnp.float32)
    top = jnp.max(logits, axis=1, keepdims=True)
    total = jnp.sum(jnp.exp(logits - top), axis=1)
    lse = top[:, 0] + jnp.log(total)
    picked = jnp.take_along_axis(logits, targets[:, None], axis=1)[:, 0]
    keep = discount * (1.0 - terminal.astype(jnp.float32))
    next_value = jnp.concatenate([lse[1:], jnp.zeros((1,), jnp.float32)])
    rewards = picked - keep * next_value
    carried = jnp.concatenate([jnp.zeros((1,), jnp.float32), (keep * cotangent)[:-1]])
    probs = jnp.exp(logits - lse[:, None])
    onehot = targets[:, None] == jnp.arange(VOCAB, dtype=jnp.int32)[None, :]
    dlogits = (jnp.where(onehot, cotangent[:, None], 0.0) - carried[:, None] * probs).astype(jnp.bfloat16)
    hidden_grad = jnp.dot(dlogits, head_weight, preferred_element_type=jnp.float32).astype(jnp.bfloat16)
    weight_grad = jnp.dot(dlogits.T, hidden_states, preferred_element_type=jnp.float32).astype(jnp.bfloat16)
    return rewards, hidden_grad, weight_grad
```

```python
import jax
import jax.numpy as jnp
from jax import lax
from jax.sharding import Mesh, PartitionSpec as P

discount = 0.99
f32 = jnp.float32
bf16 = jnp.bfloat16


def three_parts(value):
    high = lax.reduce_precision(value, 8, 7)
    rest = value - high
    middle = lax.reduce_precision(rest, 8, 7)
    return [high, middle, rest - middle]


def shards(hidden_states, head_weight, targets, terminal, cotangent):
    rows = head_weight.shape[0]
    tokens = targets.shape[0]
    sz = {a: lax.axis_size(a) for a in ("x", "z", "y", "c")}
    n_width = sz["y"] * sz["c"]
    n_vocab = sz["x"] * sz["z"]
    own = tokens // n_width
    half = tokens // sz["c"]
    x, z, y, c = (lax.axis_index(a) for a in ("x", "z", "y", "c"))
    first_row = (x * sz["z"] + z) * rows
    first_token = (c * sz["y"] + y) * own

    keep = discount * (1.0 - terminal.astype(f32))
    carried = jnp.concatenate([jnp.zeros((1,), f32), (keep * cotangent)[:-1]])

    with jax.named_scope("gather_hidden"):
        hidden = lax.all_gather(hidden_states, "z", axis=0, tiled=True)
        hidden = lax.all_gather(hidden, "x", axis=0, tiled=True)

    with jax.named_scope("logits"):
        partial = lax.dot_general(
            hidden, head_weight, (((1,), (1,)), ((), ())), preferred_element_type=f32
        ).astype(jnp.float16)
        pieces = lax.all_to_all(
            partial.reshape(n_width, own, rows), ("c", "y"), 0, 0, tiled=True
        )
        logits = jnp.sum(pieces.astype(f32), axis=0)

    with jax.named_scope("statistics"):
        cut = lambda v: lax.dynamic_slice(v, (first_token,), (own,))
        hit = (cut(targets) - first_row)[:, None] == jnp.arange(rows, dtype=jnp.int32)
        top = jnp.max(logits, axis=1)
        total = jnp.sum(jnp.exp(logits - top[:, None]), axis=1)
        picked = jnp.sum(jnp.where(hit, logits, 0.0), axis=1)
        mine = jnp.concatenate([top, total, picked, jnp.zeros((own,), f32)])
        every = lax.all_to_all(
            jnp.broadcast_to(mine, (n_vocab, 4 * own)), ("z", "x"), 0, 0, tiled=True
        ).reshape(n_vocab, 4, own)
        top_all = jnp.max(every[:, 0], axis=0)
        total_all = jnp.sum(every[:, 1] * jnp.exp(every[:, 0] - top_all), axis=0)
        lse = top_all + jnp.log(total_all)
        picked = jnp.sum(every[:, 2], axis=0)

    with jax.named_scope("gather_dlogits"):
        dlogits = jnp.where(hit, cut(cotangent)[:, None], 0.0) - cut(carried)[
            :, None
        ] * jnp.exp(logits - lse[:, None])
        extra = jnp.stack(three_parts(lse) + three_parts(picked), axis=1)
        extra = jnp.pad(extra, ((0, 0), (0, 128 - extra.shape[1])))
        sent = jnp.concatenate([dlogits.astype(bf16), extra.astype(bf16)], axis=1)
        near = lax.all_gather(sent, "y", axis=0, tiled=True)
        far = lax.ppermute(near, "c", [(0, 1), (1, 0)])

    with jax.named_scope("products"):
        is_low = c == 0
        outer = (((0,), (0,)), ((), ()))
        low_h, high_h = hidden[:half], hidden[half:]
        near_h = jnp.where(is_low, low_h, high_h)
        far_h = jnp.where(is_low, high_h, low_h)
        near_d, far_d = near[:, :rows], far[:, :rows]
        near_g = jnp.dot(near_d, head_weight, preferred_element_type=f32).astype(bf16)
        far_g = jnp.dot(far_d, head_weight, preferred_element_type=f32).astype(bf16)
        weight_grad = (
            lax.dot_general(near_d, near_h, outer, preferred_element_type=f32)
            + lax.dot_general(far_d, far_h, outer, preferred_element_type=f32)
        ).astype(bf16)
        grad = jnp.concatenate(
            [jnp.where(is_low, near_g, far_g), jnp.where(is_low, far_g, near_g)]
        )

    with jax.named_scope("scatter_hidden_grad"):
        width = grad.shape[1]
        grad = lax.all_to_all(
            grad.reshape(sz["x"], tokens // sz["x"], width), "x", 0, 0, tiled=True
        )
        grad = jnp.sum(grad.astype(f32), axis=0).astype(bf16)
        grad = lax.all_to_all(
            grad.reshape(sz["z"], tokens // n_vocab, width), "z", 0, 0, tiled=True
        )
        hidden_grad = jnp.sum(grad.astype(f32), axis=0).astype(bf16)

    with jax.named_scope("rewards"):
        near_s = near[:, rows : rows + 8].astype(f32)
        far_s = far[:, rows : rows + 8].astype(f32)
        stats = jnp.concatenate(
            [jnp.where(is_low, near_s, far_s), jnp.where(is_low, far_s, near_s)]
        )
        lse_all = stats[:, 0] + stats[:, 1] + stats[:, 2]
        picked_all = stats[:, 3] + stats[:, 4] + stats[:, 5]
        next_value = jnp.concatenate([lse_all[1:], jnp.zeros((1,), f32)])
        rewards = picked_all - keep * next_value
    return (rewards, hidden_grad, weight_grad)


def solution(mesh):
    fine = Mesh(mesh.devices.reshape(4, 16, 4, 2), ("x", "z", "y", "c"))
    block = P(("x", "z"), ("y", "c"))
    return jax.shard_map(
        shards,
        mesh=fine,
        in_specs=(block, block, P(), P(), P()),
        out_specs=(P(), block, block),
        check_vma=False,
    )
```

```python
import jax
import jax.numpy as jnp
from jax import lax
from jax.sharding import Mesh, PartitionSpec as P

discount = 0.99
f32 = jnp.float32
bf16 = jnp.bfloat16
f16 = jnp.float16


def three_parts(value):
    high = lax.reduce_precision(value, 8, 7)
    rest = value - high
    middle = lax.reduce_precision(rest, 8, 7)
    return [high, middle, rest - middle]


def spread(block, axis):
    copies = jnp.broadcast_to(block, (lax.axis_size(axis), *block.shape))
    copies = lax.all_to_all(copies, axis, 0, 0, tiled=True)
    return copies.reshape(-1, block.shape[-1])


def shards(hidden_states, head_weight, targets, terminal, cotangent):
    rows = head_weight.shape[0]
    tokens = targets.shape[0]
    sz = {a: lax.axis_size(a) for a in ("x", "z", "y", "c")}
    n_width = sz["y"] * sz["c"]
    n_vocab = sz["x"] * sz["z"]
    own = tokens // n_width
    half = tokens // sz["c"]
    x, z, y, c = (lax.axis_index(a) for a in ("x", "z", "y", "c"))
    first_row = (x * sz["z"] + z) * rows
    first_token = (c * sz["y"] + y) * own

    keep = discount * (1.0 - terminal.astype(f32))
    carried = jnp.concatenate([jnp.zeros((1,), f32), (keep * cotangent)[:-1]])

    with jax.named_scope("gather_hidden"):
        hidden = spread(spread(hidden_states, "z"), "x")
        hidden = hidden.reshape(tokens, hidden.shape[-1])

    with jax.named_scope("logits"):
        is_low = c == 0
        near_h = lax.dynamic_slice_in_dim(hidden, c * half, half)
        far_h = lax.dynamic_slice_in_dim(hidden, (1 - c) * half, half)
        inner = (((1,), (1,)), ((), ()))
        far_l = lax.dot_general(far_h, head_weight, inner, preferred_element_type=f32)
        far_l = lax.ppermute(far_l.astype(f16), "c", [(0, 1), (1, 0)])
        near_l = lax.dot_general(near_h, head_weight, inner, preferred_element_type=f32)
        chip_l = (near_l + far_l.astype(f32)).astype(f16)
        pieces = lax.all_to_all(chip_l.reshape(sz["y"], own, rows), "y", 0, 0, tiled=True)
        logits = jnp.sum(pieces.astype(f32), axis=0)

    with jax.named_scope("statistics"):
        cut = lambda v: lax.dynamic_slice(v, (first_token,), (own,))
        hit = (cut(targets) - first_row)[:, None] == jnp.arange(rows, dtype=jnp.int32)
        top = jnp.max(logits, axis=1)
        total = jnp.sum(jnp.exp(logits - top[:, None]), axis=1)
        picked = jnp.sum(jnp.where(hit, logits, 0.0), axis=1)
        mine = jnp.concatenate([top + jnp.log(total), picked])
        every = lax.all_to_all(
            jnp.broadcast_to(mine, (n_vocab, 2 * own)), ("z", "x"), 0, 0, tiled=True
        )
        top = jnp.max(every[:, :own], axis=0)
        lse = top + jnp.log(jnp.sum(jnp.exp(every[:, :own] - top), axis=0))
        picked = jnp.sum(every[:, own:], axis=0)

    with jax.named_scope("gather_dlogits"):
        dlogits = jnp.where(hit, cut(cotangent)[:, None], 0.0) - cut(carried)[
            :, None
        ] * jnp.exp(logits - lse[:, None])
        extra = jnp.stack(three_parts(lse) + three_parts(picked), axis=1)
        extra = jnp.pad(extra, ((0, 0), (0, 128 - extra.shape[1])))
        sent = jnp.concatenate([dlogits.astype(bf16), extra.astype(bf16)], axis=1)
        near = lax.all_gather(sent, "y", axis=0, tiled=True)
        far = lax.ppermute(near, "c", [(0, 1), (1, 0)])

    with jax.named_scope("products"):
        outer = (((0,), (0,)), ((), ()))
        near_d, far_d = near[:, :rows], far[:, :rows]
        near_g = jnp.dot(near_d, head_weight, preferred_element_type=f32).astype(f16)
        far_g = jnp.dot(far_d, head_weight, preferred_element_type=f32).astype(f16)
        weight_grad = (
            lax.dot_general(near_d, near_h, outer, preferred_element_type=f32)
            + lax.dot_general(far_d, far_h, outer, preferred_element_type=f32)
        ).astype(bf16)
        grad = jnp.concatenate(
            [jnp.where(is_low, near_g, far_g), jnp.where(is_low, far_g, near_g)]
        )

    with jax.named_scope("scatter_hidden_grad"):
        width = grad.shape[1]
        grad = lax.all_to_all(
            grad.reshape(sz["x"], tokens // sz["x"], width), "x", 0, 0, tiled=True
        )
        grad = jnp.sum(grad.astype(f32), axis=0).astype(f16)
        grad = lax.all_to_all(
            grad.reshape(sz["z"], tokens // n_vocab, width), "z", 0, 0, tiled=True
        )
        hidden_grad = jnp.sum(grad.astype(f32), axis=0).astype(bf16)

    with jax.named_scope("rewards"):
        near_s = near[:, rows : rows + 8].astype(f32)
        far_s = far[:, rows : rows + 8].astype(f32)
        stats = jnp.concatenate(
            [jnp.where(is_low, near_s, far_s), jnp.where(is_low, far_s, near_s)]
        )
        lse_all = stats[:, 0] + stats[:, 1] + stats[:, 2]
        picked_all = stats[:, 3] + stats[:, 4] + stats[:, 5]
        next_value = jnp.concatenate([lse_all[1:], jnp.zeros((1,), f32)])
        rewards = picked_all - keep * next_value
    return (rewards, hidden_grad, weight_grad)


def solution(mesh):
    fine = Mesh(mesh.devices.reshape(4, 16, 4, 2), ("x", "z", "y", "c"))
    block = P(("x", "z"), ("y", "c"))
    return jax.shard_map(
        shards,
        mesh=fine,
        in_specs=(block, block, P(), P(), P()),
        out_specs=(P(), block, block),
        check_vma=False,
    )
```

```python
import jax
import jax.numpy as jnp
from jax import lax
from jax.sharding import Mesh, PartitionSpec as P

discount = 0.99
f32 = jnp.float32
bf16 = jnp.bfloat16
f16 = jnp.float16


def three_parts(value):
    high = lax.reduce_precision(value, 8, 7)
    rest = value - high
    middle = lax.reduce_precision(rest, 8, 7)
    return [high, middle, rest - middle]


def spread(block, axis):
    copies = jnp.broadcast_to(block, (lax.axis_size(axis), *block.shape))
    copies = lax.all_to_all(copies, axis, 0, 0, tiled=True)
    return copies.reshape(-1, block.shape[-1])


def shards(hidden_states, head_weight, targets, terminal, cotangent):
    rows = head_weight.shape[0]
    tokens = targets.shape[0]
    sz = {a: lax.axis_size(a) for a in ("x", "z", "y", "c")}
    n_width = sz["y"] * sz["c"]
    n_vocab = sz["x"] * sz["z"]
    own = tokens // n_width
    half = tokens // sz["c"]
    part = (sz["c"], sz["x"], own)
    x, z, y, c = (lax.axis_index(a) for a in ("x", "z", "y", "c"))
    first_row = (x * sz["z"] + z) * rows
    first_token = (y * sz["c"] + c) * own
    width = head_weight.shape[1]
    is_low = c == 0
    swap = lambda v: lax.ppermute(v, "c", [(0, 1), (1, 0)])

    with jax.named_scope("partner_weight"):
        other_weight = swap(head_weight)
        low_weight = jnp.where(is_low, head_weight, other_weight)
        high_weight = jnp.where(is_low, other_weight, head_weight)

    keep = discount * (1.0 - terminal.astype(f32))
    carried = jnp.concatenate([jnp.zeros((1,), f32), (keep * cotangent)[:-1]])

    with jax.named_scope("gather_hidden"):
        hidden = spread(hidden_states, "z").reshape(sz["c"], 1, own, width)
        hidden = jnp.broadcast_to(hidden, (*part, width)).reshape(-1, own, width)
        hidden = lax.all_to_all(hidden, ("c", "x"), 0, 0, tiled=True)
        hidden = hidden.reshape(sz["c"], half, width)
        near_h = lax.dynamic_index_in_dim(hidden, c, keepdims=False)
        far_h = swap(lax.dynamic_index_in_dim(hidden, 1 - c, keepdims=False))

    with jax.named_scope("logits"):
        inner = (((1,), (1,)), ((), ()))
        chip_l = (
            lax.dot_general(hidden[0], low_weight, inner, preferred_element_type=f32)
            + lax.dot_general(hidden[1], high_weight, inner, preferred_element_type=f32)
        ).astype(f16)
        pieces = lax.all_to_all(chip_l.reshape(sz["y"], own, rows), "y", 0, 0, tiled=True)
        logits = jnp.sum(pieces.astype(f32), axis=0)

    with jax.named_scope("statistics"):
        cut = lambda v: lax.dynamic_slice(v, (first_token,), (own,))
        hit = (cut(targets) - first_row)[:, None] == jnp.arange(rows, dtype=jnp.int32)
        top = jnp.max(logits, axis=1)
        total = jnp.sum(jnp.exp(logits - top[:, None]), axis=1)
        picked = jnp.sum(jnp.where(hit, logits, 0.0), axis=1)
        mine = jnp.concatenate([top + jnp.log(total), picked])
        every = lax.all_to_all(
            jnp.broadcast_to(mine, (n_vocab, 2 * own)), ("z", "x"), 0, 0, tiled=True
        )
        top = jnp.max(every[:, :own], axis=0)
        lse = top + jnp.log(jnp.sum(jnp.exp(every[:, :own] - top), axis=0))
        picked = jnp.sum(every[:, own:], axis=0)

    with jax.named_scope("gather_dlogits"):
        dlogits = jnp.where(hit, cut(cotangent)[:, None], 0.0) - cut(carried)[
            :, None
        ] * jnp.exp(logits - lse[:, None])
        extra = jnp.stack(three_parts(lse) + three_parts(picked), axis=1)
        extra = jnp.pad(extra, ((0, 0), (0, 128 - extra.shape[1])))
        sent = jnp.concatenate([dlogits.astype(bf16), extra.astype(bf16)], axis=1)
        near = lax.all_gather(sent, "y", axis=0, tiled=True)
        far = swap(near)

    with jax.named_scope("products"):
        outer = (((0,), (0,)), ((), ()))
        near_d, far_d = near[:, :rows], far[:, :rows]
        grad = jnp.stack(
            [
                jnp.dot(near_d, low_weight, preferred_element_type=f32).astype(f16),
                jnp.dot(near_d, high_weight, preferred_element_type=f32).astype(f16),
            ]
        )
        weight_grad = (
            lax.dot_general(near_d, near_h, outer, preferred_element_type=f32)
            + lax.dot_general(far_d, far_h, outer, preferred_element_type=f32)
        ).astype(bf16)

    with jax.named_scope("scatter_hidden_grad"):
        grad = lax.all_to_all(grad.reshape(-1, own, width), ("c", "x"), 0, 0, tiled=True)
        grad = jnp.sum(grad.reshape(*part, width).astype(f32), axis=1).astype(f16)
        grad = lax.all_to_all(
            grad.reshape(sz["z"], tokens // n_vocab, width), "z", 0, 0, tiled=True
        )
        hidden_grad = jnp.sum(grad.astype(f32), axis=0).astype(bf16)

    with jax.named_scope("rewards"):
        near_s = near[:, rows : rows + 8].astype(f32)
        far_s = far[:, rows : rows + 8].astype(f32)
        near_s, far_s = (v.reshape(sz["x"], own, -1) for v in (near_s, far_s))
        low_s = jnp.where(is_low, near_s, far_s)
        high_s = jnp.where(is_low, far_s, near_s)
        stats = jnp.stack([low_s, high_s], axis=1).reshape(tokens, -1)
        lse_all = stats[:, 0] + stats[:, 1] + stats[:, 2]
        picked_all = stats[:, 3] + stats[:, 4] + stats[:, 5]
        next_value = jnp.concatenate([lse_all[1:], jnp.zeros((1,), f32)])
        rewards = picked_all - keep * next_value
    return (rewards, hidden_grad, weight_grad)


def solution(mesh):
    fine = Mesh(mesh.devices.reshape(4, 16, 4, 2), ("x", "z", "y", "c"))
    block = P(("x", "z"), ("y", "c"))
    return jax.shard_map(
        shards,
        mesh=fine,
        in_specs=(block, block, P(), P(), P()),
        out_specs=(P(), block, block),
        check_vma=False,
    )
```

```python
import jax
import jax.numpy as jnp
from jax import lax
from jax.sharding import Mesh, PartitionSpec as P

discount = 0.99
f32 = jnp.float32
bf16 = jnp.bfloat16
f16 = jnp.float16


def spread(block, axis):
    copies = jnp.broadcast_to(block, (lax.axis_size(axis), *block.shape))
    copies = lax.all_to_all(copies, axis, 0, 0, tiled=True)
    return copies.reshape(-1, block.shape[-1])


def shards(hidden_states, head_weight, targets, terminal, cotangent):
    rows, width = head_weight.shape
    tokens = targets.shape[0]
    sz = {a: lax.axis_size(a) for a in ("x", "z", "y", "c")}
    n_width = sz["y"] * sz["c"]
    n_vocab = sz["x"] * sz["z"]
    own = tokens // n_width
    half = tokens // sz["c"]
    x, z, y, c = (lax.axis_index(a) for a in ("x", "z", "y", "c"))
    first_row = (x * sz["z"] + z) * rows
    first_token = (c * sz["y"] + y) * own
    is_low = c == 0
    swap = lambda v: lax.ppermute(v, "c", [(0, 1), (1, 0)])
    turn = lambda v, axis: lax.all_to_all(v, axis, 0, 0, tiled=True)
    cut = lambda v: lax.dynamic_slice(v, (first_token,), (own,))

    keep = discount * (1.0 - terminal.astype(f32))
    carried = jnp.concatenate([jnp.zeros((1,), f32), (keep * cotangent)[:-1]])
    column = jnp.arange(rows, dtype=jnp.int32)

    with jax.named_scope("gather_hidden"):
        hidden = spread(spread(hidden_states, "z"), "x")

    with jax.named_scope("logits"):
        near_h = lax.dynamic_slice_in_dim(hidden, c * half, half)
        far_h = lax.dynamic_slice_in_dim(hidden, (1 - c) * half, half)
        inner = (((1,), (1,)), ((), ()))
        far_l = lax.dot_general(far_h, head_weight, inner, preferred_element_type=f32)
        far_l = swap(far_l.astype(f16))
        near_l = lax.dot_general(near_h, head_weight, inner, preferred_element_type=f32)
        chip_l = (near_l + far_l.astype(f32)).astype(f16)
        pieces = turn(chip_l.reshape(sz["y"], own, rows), "y")
        logits = jnp.sum(pieces.astype(f32), axis=0)

    with jax.named_scope("own_statistics"):
        hit = (cut(targets) - first_row)[:, None] == column
        own_top = jnp.max(logits, axis=1)
        raised = jnp.exp(logits - own_top[:, None])
        picked = jnp.sum(jnp.where(hit, logits, 0.0), axis=1)
        mine = jnp.concatenate([own_top + jnp.log(jnp.sum(raised, axis=1)), picked])
        mine = jnp.broadcast_to(mine, (n_vocab, 2 * own))

    with jax.named_scope("gather_raised"):
        near = lax.all_gather(raised.astype(bf16), "y", axis=0, tiled=True)
        far = swap(near)
        raised = jnp.concatenate([jnp.where(is_low, near, far), jnp.where(is_low, far, near)])

    with jax.named_scope("statistics"):
        every = turn(mine, ("z", "x"))
        top = jnp.max(every[:, :own], axis=0)
        lse = top + jnp.log(jnp.sum(jnp.exp(every[:, :own] - top), axis=0))
        picked = jnp.sum(every[:, own:], axis=0)
        parts = jnp.concatenate([lse, picked, jnp.exp(own_top - lse), lse])
        parts, _ = lax.optimization_barrier((parts, near))
        parts = turn(jnp.broadcast_to(parts, (n_width, 4 * own)), ("c", "y"))
        lse, picked, factor, _ = (
            parts[:, i * own : (i + 1) * own].reshape(tokens) for i in range(4)
        )

    with jax.named_scope("products"):
        hit_all = (targets - first_row)[:, None] == column
        dlogits = jnp.where(hit_all, cotangent[:, None], 0.0)
        dlogits = (dlogits - (carried * factor)[:, None] * raised.astype(f32)).astype(bf16)
        grad = jnp.dot(dlogits, head_weight, preferred_element_type=f32).astype(f16)
        outer = (((0,), (0,)), ((), ()))
        weight_grad = lax.dot_general(dlogits, hidden, outer, preferred_element_type=f32)
        weight_grad = weight_grad.astype(bf16)

    with jax.named_scope("scatter_hidden_grad"):
        grad = turn(grad.reshape(sz["x"], -1, width), "x")
        grad = jnp.sum(grad.astype(f32), axis=0).astype(f16)
        grad = turn(grad.reshape(sz["z"], -1, width), "z")
        hidden_grad = jnp.sum(grad.astype(f32), axis=0).astype(bf16)

    with jax.named_scope("rewards"):
        next_value = jnp.concatenate([lse[1:], jnp.zeros((1,), f32)])
        rewards = picked - keep * next_value
    return (rewards, hidden_grad, weight_grad)


def solution(mesh):
    fine = Mesh(mesh.devices.reshape(4, 16, 4, 2), ("x", "z", "y", "c"))
    block = P(("x", "z"), ("y", "c"))
    return jax.shard_map(
        shards,
        mesh=fine,
        in_specs=(block, block, P(), P(), P()),
        out_specs=(P(), block, block),
        check_vma=False,
    )
```

```python
import jax
import jax.numpy as jnp
from jax import lax
from jax.sharding import Mesh, PartitionSpec as P

discount = 0.99
f32 = jnp.float32
bf16 = jnp.bfloat16
f16 = jnp.float16


def spread(block, axis):
    copies = jnp.broadcast_to(block, (lax.axis_size(axis), *block.shape))
    copies = lax.all_to_all(copies, axis, 0, 0, tiled=True)
    return copies.reshape(-1, block.shape[-1])


def gather_by_pairs(block, axis):
    me = lax.axis_index(axis)
    by_pair = [block]
    for other in range(1, 4):
        by_pair.append(lax.ppermute(block, axis, [(i, i ^ other) for i in range(4)]))
    odd, late = me % 2 == 1, me >= 2
    even_first = [jnp.where(odd, by_pair[i ^ 1], by_pair[i]) for i in range(4)]
    return jnp.stack([jnp.where(late, even_first[i ^ 2], even_first[i]) for i in range(4)])


def shards(hidden_states, head_weight, targets, terminal, cotangent):
    rows, width = head_weight.shape
    tokens = targets.shape[0]
    sz = {a: lax.axis_size(a) for a in ("x", "z", "y", "c")}
    n_width = sz["y"] * sz["c"]
    n_vocab = sz["x"] * sz["z"]
    own = tokens // n_width
    half = tokens // sz["c"]
    x, z, y, c = (lax.axis_index(a) for a in ("x", "z", "y", "c"))
    first_row = (x * sz["z"] + z) * rows
    first_token = (c * sz["y"] + y) * own
    is_low = c == 0
    swap = lambda v: lax.ppermute(v, "c", [(0, 1), (1, 0)])
    turn = lambda v, axis: lax.all_to_all(v, axis, 0, 0, tiled=True)
    cut = lambda v: lax.dynamic_slice(v, (first_token,), (own,))

    keep = discount * (1.0 - terminal.astype(f32))
    carried = jnp.concatenate([jnp.zeros((1,), f32), (keep * cotangent)[:-1]])
    column = jnp.arange(rows, dtype=jnp.int32)

    with jax.named_scope("gather_hidden"):
        hidden = spread(spread(hidden_states, "z"), "x")

    with jax.named_scope("logits"):
        near_h = lax.dynamic_slice_in_dim(hidden, c * half, half)
        far_h = lax.dynamic_slice_in_dim(hidden, (1 - c) * half, half)
        inner = (((1,), (1,)), ((), ()))
        far_l = lax.dot_general(far_h, head_weight, inner, preferred_element_type=f32)
        far_l = swap(far_l.astype(f16))
        near_l = lax.dot_general(near_h, head_weight, inner, preferred_element_type=f32)
        near_l = lax.optimization_barrier(near_l)
        chip_l = (near_l + far_l.astype(f32)).astype(f16)
        pieces = turn(chip_l.reshape(sz["y"], own, rows), "y")
        logits = jnp.sum(pieces.astype(f32), axis=0)

    with jax.named_scope("own_statistics"):
        hit = (cut(targets) - first_row)[:, None] == column
        own_top = jnp.max(logits, axis=1)
        raised = jnp.exp(logits - own_top[:, None])
        picked = jnp.sum(jnp.where(hit, logits, 0.0), axis=1)
        mine = jnp.concatenate([own_top + jnp.log(jnp.sum(raised, axis=1)), picked])
        mine = jnp.broadcast_to(mine, (n_vocab, 2 * own))

    with jax.named_scope("gather_raised"):
        near = gather_by_pairs(raised.astype(bf16), "y").reshape(half, rows)
        far = swap(near)
        raised = jnp.concatenate([jnp.where(is_low, near, far), jnp.where(is_low, far, near)])

    with jax.named_scope("statistics"):
        every = turn(mine, ("z", "x"))
        top = jnp.max(every[:, :own], axis=0)
        lse = top + jnp.log(jnp.sum(jnp.exp(every[:, :own] - top), axis=0))
        picked = jnp.sum(every[:, own:], axis=0)
        parts = jnp.concatenate([lse, picked, jnp.exp(own_top - lse), lse])
        parts, _ = lax.optimization_barrier((parts, near))
        parts = turn(jnp.broadcast_to(parts, (n_width, 4 * own)), ("c", "y"))
        lse, picked, factor, _ = (
            parts[:, i * own : (i + 1) * own].reshape(tokens) for i in range(4)
        )

    with jax.named_scope("products"):
        hit_all = (targets - first_row)[:, None] == column
        dlogits = jnp.where(hit_all, cotangent[:, None], 0.0)
        dlogits = (dlogits - (carried * factor)[:, None] * raised.astype(f32)).astype(bf16)
        grad = jnp.dot(dlogits, head_weight, preferred_element_type=f32).astype(f16)
        outer = (((0,), (0,)), ((), ()))
        weight_grad = lax.dot_general(dlogits, hidden, outer, preferred_element_type=f32)
        weight_grad = weight_grad.astype(bf16)

    with jax.named_scope("scatter_hidden_grad"):
        grad = turn(grad.reshape(sz["x"], -1, width), "x")
        grad = jnp.sum(grad.astype(f32), axis=0).astype(f16)
        grad = turn(grad.reshape(sz["z"], -1, width), "z")
        hidden_grad = jnp.sum(grad.astype(f32), axis=0).astype(bf16)

    with jax.named_scope("rewards"):
        next_value = jnp.concatenate([lse[1:], jnp.zeros((1,), f32)])
        rewards = picked - keep * next_value
    return (rewards, hidden_grad, weight_grad)


def solution(mesh):
    fine = Mesh(mesh.devices.reshape(4, 16, 4, 2), ("x", "z", "y", "c"))
    block = P(("x", "z"), ("y", "c"))
    return jax.shard_map(
        shards,
        mesh=fine,
        in_specs=(block, block, P(), P(), P()),
        out_specs=(P(), block, block),
        check_vma=False,
    )
```

```python
import jax
import jax.numpy as jnp
from jax import lax
from jax.sharding import Mesh, PartitionSpec as P

discount = 0.99
f32 = jnp.float32
bf16 = jnp.bfloat16
f16 = jnp.float16


def spread(block, axis):
    copies = jnp.broadcast_to(block, (lax.axis_size(axis), *block.shape))
    copies = lax.all_to_all(copies, axis, 0, 0, tiled=True)
    return copies.reshape(-1, block.shape[-1])


def shards(hidden_states, head_weight, targets, terminal, cotangent):
    rows, width = head_weight.shape
    tokens = targets.shape[0]
    sz = {a: lax.axis_size(a) for a in ("x", "z", "y", "c")}
    n_width = sz["y"] * sz["c"]
    n_vocab = sz["x"] * sz["z"]
    own = tokens // n_width
    half = tokens // sz["c"]
    x, z, y, c = (lax.axis_index(a) for a in ("x", "z", "y", "c"))
    first_row = (x * sz["z"] + z) * rows
    first_token = (c * sz["y"] + y) * own
    is_low = c == 0
    swap = lambda v: lax.ppermute(v, "c", [(0, 1), (1, 0)])
    turn = lambda v, axis: lax.all_to_all(v, axis, 0, 0, tiled=True)
    cut = lambda v: lax.dynamic_slice(v, (first_token,), (own,))

    keep = discount * (1.0 - terminal.astype(f32))
    carried = jnp.concatenate([jnp.zeros((1,), f32), (keep * cotangent)[:-1]])
    column = jnp.arange(rows, dtype=jnp.int32)

    with jax.named_scope("gather_hidden"):
        hidden = spread(spread(hidden_states, "z"), "x")

    with jax.named_scope("logits"):
        near_h = lax.dynamic_slice_in_dim(hidden, c * half, half)
        far_h = lax.dynamic_slice_in_dim(hidden, (1 - c) * half, half)
        inner = (((1,), (1,)), ((), ()))
        far_l = lax.dot_general(far_h, head_weight, inner, preferred_element_type=f32)
        far_l = swap(far_l.astype(f16))
        near_l = lax.dot_general(near_h, head_weight, inner, preferred_element_type=f32)
        near_l = lax.optimization_barrier(near_l)
        chip_l = (near_l + far_l.astype(f32)).astype(f16)
        pieces = turn(chip_l.reshape(sz["y"], own, rows), "y")
        logits = jnp.sum(pieces.astype(f32), axis=0)

    with jax.named_scope("own_statistics"):
        hit = (cut(targets) - first_row)[:, None] == column
        own_top = jnp.max(logits, axis=1)
        raised = jnp.exp(logits - own_top[:, None])
        picked = jnp.sum(jnp.where(hit, logits, 0.0), axis=1)
        mine = jnp.concatenate([own_top + jnp.log(jnp.sum(raised, axis=1)), picked])
        mine = jnp.broadcast_to(mine, (n_vocab, 2 * own))

    with jax.named_scope("gather_raised"):
        near = lax.all_gather(raised.astype(bf16), "y", axis=0, tiled=True)
        far = swap(near)
        raised = jnp.concatenate([jnp.where(is_low, near, far), jnp.where(is_low, far, near)])

    with jax.named_scope("statistics"):
        every = turn(mine, ("z", "x"))
        top = jnp.max(every[:, :own], axis=0)
        lse = top + jnp.log(jnp.sum(jnp.exp(every[:, :own] - top), axis=0))
        picked = jnp.sum(every[:, own:], axis=0)
        parts = jnp.concatenate([lse, picked, jnp.exp(own_top - lse), lse])
        parts, _ = lax.optimization_barrier((parts, near))
        parts = turn(jnp.broadcast_to(parts, (n_width, 4 * own)), ("c", "y"))
        lse, picked, factor, _ = (
            parts[:, i * own : (i + 1) * own].reshape(tokens) for i in range(4)
        )

    with jax.named_scope("products"):
        hit_all = (targets - first_row)[:, None] == column
        dlogits = jnp.where(hit_all, cotangent[:, None], 0.0)
        dlogits = (dlogits - (carried * factor)[:, None] * raised.astype(f32)).astype(bf16)
        grad = jnp.dot(dlogits, head_weight, preferred_element_type=f32).astype(f16)
        outer = (((0,), (0,)), ((), ()))
        weight_grad = lax.dot_general(dlogits, hidden, outer, preferred_element_type=f32)
        weight_grad = weight_grad.astype(bf16)

    with jax.named_scope("scatter_hidden_grad"):
        grad = turn(grad.reshape(sz["x"], -1, width), "x")
        grad = jnp.sum(grad.astype(f32), axis=0).astype(f16)
        grad = turn(grad.reshape(sz["z"], -1, width), "z")
        hidden_grad = jnp.sum(grad.astype(f32), axis=0).astype(bf16)

    with jax.named_scope("rewards"):
        next_value = jnp.concatenate([lse[1:], jnp.zeros((1,), f32)])
        rewards = picked - keep * next_value
    return (rewards, hidden_grad, weight_grad)


def solution(mesh):
    fine = Mesh(mesh.devices.reshape(4, 16, 4, 2), ("x", "z", "y", "c"))
    block = P(("x", "z"), ("y", "c"))
    return jax.shard_map(
        shards,
        mesh=fine,
        in_specs=(block, block, P(), P(), P()),
        out_specs=(P(), block, block),
        check_vma=False,
    )
```

```python
import jax
import jax.numpy as jnp
from jax import lax
from jax.sharding import Mesh, PartitionSpec as P

discount = 0.99
raise_logits = 8.0
raise_grad = 65536.0
f32 = jnp.float32
bf16 = jnp.bfloat16
f16 = jnp.float16


def spread(block, axis):
    copies = jnp.broadcast_to(block, (lax.axis_size(axis), *block.shape))
    copies = lax.all_to_all(copies, axis, 0, 0, tiled=True)
    return copies.reshape(-1, block.shape[-1])


def shards(hidden_states, head_weight, targets, terminal, cotangent):
    rows, width = head_weight.shape
    tokens = targets.shape[0]
    sz = {a: lax.axis_size(a) for a in ("x", "z", "y", "c")}
    n_width = sz["y"] * sz["c"]
    n_vocab = sz["x"] * sz["z"]
    own = tokens // n_width
    half = tokens // sz["c"]
    x, z, y, c = (lax.axis_index(a) for a in ("x", "z", "y", "c"))
    first_row = (x * sz["z"] + z) * rows
    first_token = (c * sz["y"] + y) * own
    is_low = c == 0
    swap = lambda v: lax.ppermute(v, "c", [(0, 1), (1, 0)])
    turn = lambda v, axis: lax.all_to_all(v, axis, 0, 0, tiled=True)
    cut = lambda v: lax.dynamic_slice(v, (first_token,), (own,))

    keep = discount * (1.0 - terminal.astype(f32))
    carried = jnp.concatenate([jnp.zeros((1,), f32), (keep * cotangent)[:-1]])
    unit = jnp.maximum(jnp.max(jnp.abs(cotangent)), 1e-30)
    column = jnp.arange(rows, dtype=jnp.int32)

    with jax.named_scope("gather_hidden"):
        hidden = spread(spread(hidden_states, "z"), "x")

    with jax.named_scope("logits"):
        near_h = lax.dynamic_slice_in_dim(hidden, c * half, half)
        far_h = lax.dynamic_slice_in_dim(hidden, (1 - c) * half, half)
        inner = (((1,), (1,)), ((), ()))
        far_l = lax.dot_general(far_h, head_weight, inner, preferred_element_type=f32)
        far_l = swap((far_l * raise_logits).astype(f16))
        near_l = lax.dot_general(near_h, head_weight, inner, preferred_element_type=f32)
        near_l = lax.optimization_barrier(near_l)
        chip_l = (near_l * raise_logits + far_l.astype(f32)).astype(f16)
        pieces = turn(chip_l.reshape(sz["y"], own, rows), "y")
        logits = jnp.sum(pieces.astype(f32), axis=0) * (1.0 / raise_logits)

    with jax.named_scope("own_statistics"):
        hit = (cut(targets) - first_row)[:, None] == column
        own_top = jnp.max(logits, axis=1)
        raised = jnp.exp(logits - own_top[:, None])
        picked = jnp.sum(jnp.where(hit, logits, 0.0), axis=1)
        mine = jnp.concatenate([own_top + jnp.log(jnp.sum(raised, axis=1)), picked])
        mine = jnp.broadcast_to(mine, (n_vocab, 2 * own))

    with jax.named_scope("gather_raised"):
        near = lax.all_gather(raised.astype(bf16), "y", axis=0, tiled=True)
        far = swap(near)
        raised = jnp.concatenate([jnp.where(is_low, near, far), jnp.where(is_low, far, near)])

    with jax.named_scope("statistics"):
        every = turn(mine, ("z", "x"))
        top = jnp.max(every[:, :own], axis=0)
        lse = top + jnp.log(jnp.sum(jnp.exp(every[:, :own] - top), axis=0))
        picked = jnp.sum(every[:, own:], axis=0)
        parts = jnp.concatenate([lse, picked, jnp.exp(own_top - lse), lse])
        parts, _ = lax.optimization_barrier((parts, near))
        parts = turn(jnp.broadcast_to(parts, (n_width, 4 * own)), ("c", "y"))
        lse, picked, factor, _ = (
            parts[:, i * own : (i + 1) * own].reshape(tokens) for i in range(4)
        )

    with jax.named_scope("products"):
        hit_all = (targets - first_row)[:, None] == column
        dlogits = jnp.where(hit_all, cotangent[:, None], 0.0)
        dlogits = (dlogits - (carried * factor)[:, None] * raised.astype(f32)).astype(bf16)
        grad = jnp.dot(dlogits, head_weight, preferred_element_type=f32)
        grad = (grad * (raise_grad / unit)).astype(f16)
        outer = (((0,), (0,)), ((), ()))
        weight_grad = lax.dot_general(dlogits, hidden, outer, preferred_element_type=f32)
        weight_grad = weight_grad.astype(bf16)

    with jax.named_scope("scatter_hidden_grad"):
        grad = turn(grad.reshape(sz["x"], -1, width), "x")
        grad = jnp.sum(grad.astype(f32), axis=0).astype(f16)
        grad = turn(grad.reshape(sz["z"], -1, width), "z")
        hidden_grad = (jnp.sum(grad.astype(f32), axis=0) * (unit / raise_grad)).astype(bf16)

    with jax.named_scope("rewards"):
        next_value = jnp.concatenate([lse[1:], jnp.zeros((1,), f32)])
        rewards = picked - keep * next_value
    return (rewards, hidden_grad, weight_grad)


def solution(mesh):
    fine = Mesh(mesh.devices.reshape(4, 16, 4, 2), ("x", "z", "y", "c"))
    block = P(("x", "z"), ("y", "c"))
    return jax.shard_map(
        shards,
        mesh=fine,
        in_specs=(block, block, P(), P(), P()),
        out_specs=(P(), block, block),
        check_vma=False,
    )
```

```python
import jax
import jax.numpy as jnp
from jax import lax
from jax.sharding import Mesh, PartitionSpec as P

discount = 0.99
raise_logits = 8.0
raise_grad = 65536.0
f32 = jnp.float32
bf16 = jnp.bfloat16
f16 = jnp.float16


def spread(block, axis):
    copies = jnp.broadcast_to(block, (lax.axis_size(axis), *block.shape))
    copies = lax.all_to_all(copies, axis, 0, 0, tiled=True)
    return copies.reshape(-1, block.shape[-1])


def shards(hidden_states, head_weight, targets, terminal, cotangent):
    rows, width = head_weight.shape
    tokens = targets.shape[0]
    sz = {a: lax.axis_size(a) for a in ("x", "z", "y", "c")}
    n_width = sz["y"] * sz["c"]
    n_vocab = sz["x"] * sz["z"]
    own = tokens // n_width
    half = tokens // sz["c"]
    x, z, y, c = (lax.axis_index(a) for a in ("x", "z", "y", "c"))
    first_row = (x * sz["z"] + z) * rows
    first_token = (c * sz["y"] + y) * own
    is_low = c == 0
    swap = lambda v: lax.ppermute(v, "c", [(0, 1), (1, 0)])
    turn = lambda v, axis: lax.all_to_all(v, axis, 0, 0, tiled=True)
    cut = lambda v: lax.dynamic_slice(v, (first_token,), (own,))

    keep = discount * (1.0 - terminal.astype(f32))
    carried = jnp.concatenate([jnp.zeros((1,), f32), (keep * cotangent)[:-1]])
    unit = jnp.maximum(jnp.max(jnp.abs(cotangent)), 1e-30)
    down, up = lax.optimization_barrier((unit / raise_grad, raise_grad / unit))
    column = jnp.arange(rows, dtype=jnp.int32)

    with jax.named_scope("gather_hidden"):
        hidden = spread(spread(hidden_states, "z"), "x")

    with jax.named_scope("logits"):
        near_h = lax.dynamic_slice_in_dim(hidden, c * half, half)
        far_h = lax.dynamic_slice_in_dim(hidden, (1 - c) * half, half)
        inner = (((1,), (1,)), ((), ()))
        far_l = lax.dot_general(far_h, head_weight, inner, preferred_element_type=f32)
        far_l = swap((far_l * raise_logits).astype(f16))
        near_l = lax.dot_general(near_h, head_weight, inner, preferred_element_type=f32)
        near_l = lax.optimization_barrier(near_l)
        chip_l = (near_l * raise_logits + far_l.astype(f32)).astype(f16)
        pieces = turn(chip_l.reshape(sz["y"], own, rows), "y")
        logits = jnp.sum(pieces.astype(f32), axis=0) * (1.0 / raise_logits)

    with jax.named_scope("own_statistics"):
        hit = (cut(targets) - first_row)[:, None] == column
        own_top = jnp.max(logits, axis=1)
        raised = jnp.exp(logits - own_top[:, None])
        picked = jnp.sum(jnp.where(hit, logits, 0.0), axis=1)
        mine = jnp.concatenate([own_top + jnp.log(jnp.sum(raised, axis=1)), picked])
        mine = jnp.broadcast_to(mine, (n_vocab, 2 * own))

    with jax.named_scope("gather_raised"):
        near = lax.all_gather(raised.astype(bf16), "y", axis=0, tiled=True)
        far = swap(near)
        raised = jnp.concatenate([jnp.where(is_low, near, far), jnp.where(is_low, far, near)])

    with jax.named_scope("statistics"):
        every = turn(mine, ("z", "x"))
        top = jnp.max(every[:, :own], axis=0)
        lse = top + jnp.log(jnp.sum(jnp.exp(every[:, :own] - top), axis=0))
        picked = jnp.sum(every[:, own:], axis=0)
        parts = jnp.concatenate([lse, picked, cut(carried) * jnp.exp(own_top - lse), lse])
        parts, _ = lax.optimization_barrier((parts, near))
        parts = turn(jnp.broadcast_to(parts, (n_width, 4 * own)), ("c", "y"))
        lse, picked, scale, _ = (
            parts[:, i * own : (i + 1) * own].reshape(tokens) for i in range(4)
        )

    with jax.named_scope("products"):
        hit_all = (targets - first_row)[:, None] == column
        dlogits = jnp.where(hit_all, cotangent[:, None], 0.0)
        dlogits = (dlogits - scale[:, None] * raised.astype(f32)).astype(bf16)
        grad = jnp.dot(dlogits, head_weight, preferred_element_type=f32)
        grad = (grad * up).astype(f16)
        outer = (((0,), (0,)), ((), ()))
        weight_grad = lax.dot_general(dlogits, hidden, outer, preferred_element_type=f32)
        weight_grad = weight_grad.astype(bf16)

    with jax.named_scope("scatter_hidden_grad"):
        grad = turn(grad.reshape(sz["x"], -1, width), "x")
        grad = jnp.sum(grad.astype(f32), axis=0).astype(f16)
        grad = turn(grad.reshape(sz["z"], -1, width), "z")
        hidden_grad = (jnp.sum(grad.astype(f32), axis=0) * down).astype(bf16)

    with jax.named_scope("rewards"):
        next_value = jnp.concatenate([lse[1:], jnp.zeros((1,), f32)])
        rewards = picked - keep * next_value
    return (rewards, hidden_grad, weight_grad)


def solution(mesh):
    fine = Mesh(mesh.devices.reshape(4, 16, 4, 2), ("x", "z", "y", "c"))
    block = P(("x", "z"), ("y", "c"))
    return jax.shard_map(
        shards,
        mesh=fine,
        in_specs=(block, block, P(), P(), P()),
        out_specs=(P(), block, block),
        check_vma=False,
    )
```

```python
import jax
import jax.numpy as jnp
from jax import lax
from jax.sharding import Mesh, PartitionSpec as P

discount = 0.99
raise_logits = 8.0
raise_grad = 65536.0
f32 = jnp.float32
bf16 = jnp.bfloat16
f16 = jnp.float16


def spread(block, axis):
    copies = jnp.broadcast_to(block, (lax.axis_size(axis), *block.shape))
    copies = lax.all_to_all(copies, axis, 0, 0, tiled=True)
    return copies.reshape(-1, block.shape[-1])


def shards(hidden_states, head_weight, targets, terminal, cotangent):
    rows, width = head_weight.shape
    tokens = targets.shape[0]
    sz = {a: lax.axis_size(a) for a in ("x", "z", "y", "c")}
    n_width = sz["y"] * sz["c"]
    n_vocab = sz["x"] * sz["z"]
    own = tokens // n_width
    half = tokens // sz["c"]
    x, z, y, c = (lax.axis_index(a) for a in ("x", "z", "y", "c"))
    first_row = (x * sz["z"] + z) * rows
    first_token = (c * sz["y"] + y) * own
    is_low = c == 0
    swap = lambda v: lax.ppermute(v, "c", [(0, 1), (1, 0)])
    turn = lambda v, axis: lax.all_to_all(v, axis, 0, 0, tiled=True)
    cut = lambda v: lax.dynamic_slice(v, (first_token,), (own,))

    keep = discount * (1.0 - terminal.astype(f32))
    carried = jnp.concatenate([jnp.zeros((1,), f32), (keep * cotangent)[:-1]])
    unit = jnp.maximum(jnp.max(jnp.abs(cotangent)), 1e-30)
    down, up = lax.optimization_barrier((unit / raise_grad, raise_grad / unit))
    column = jnp.arange(rows, dtype=jnp.int32)

    with jax.named_scope("gather_hidden"):
        hidden = spread(spread(hidden_states, "z"), "x")

    with jax.named_scope("logits"):
        near_h = lax.dynamic_slice_in_dim(hidden, c * half, half)
        far_h = lax.dynamic_slice_in_dim(hidden, (1 - c) * half, half)
        inner = (((1,), (1,)), ((), ()))
        far_l = lax.dot_general(far_h, head_weight, inner, preferred_element_type=f32)
        far_l = swap((far_l * raise_logits).astype(f16))
        near_l = lax.dot_general(near_h, head_weight, inner, preferred_element_type=f32)
        near_l = lax.optimization_barrier(near_l)
        chip_l = (near_l * raise_logits + far_l.astype(f32)).astype(f16)
        pieces = turn(chip_l.reshape(sz["y"], own, rows), "y")
        logits = jnp.sum(pieces.astype(f32), axis=0) * (1.0 / raise_logits)

    with jax.named_scope("own_statistics"):
        hit = (cut(targets) - first_row)[:, None] == column
        own_top = jnp.max(logits, axis=1)
        raised = jnp.exp(logits - own_top[:, None])
        picked = jnp.sum(jnp.where(hit, logits, 0.0), axis=1)
        mine = jnp.concatenate([own_top + jnp.log(jnp.sum(raised, axis=1)), picked])
        mine = jnp.broadcast_to(mine, (n_vocab, 2 * own))

    with jax.named_scope("gather_raised"):
        near = lax.all_gather(raised.astype(bf16), "y", axis=0, tiled=True)

    with jax.named_scope("statistics"):
        every = turn(mine, ("z", "x"))
        top = jnp.max(every[:, :own], axis=0)
        lse = top + jnp.log(jnp.sum(jnp.exp(every[:, :own] - top), axis=0))
        picked = jnp.sum(every[:, own:], axis=0)
        parts = jnp.concatenate([lse, picked, cut(carried) * jnp.exp(own_top - lse), lse])
        parts, near = lax.optimization_barrier((parts, near))
        far = swap(near)
        raised = jnp.concatenate([jnp.where(is_low, near, far), jnp.where(is_low, far, near)])
        parts = turn(jnp.broadcast_to(parts, (n_width, 4 * own)), ("c", "y"))
        lse, picked, scale, _ = (
            parts[:, i * own : (i + 1) * own].reshape(tokens) for i in range(4)
        )

    with jax.named_scope("products"):
        hit_all = (targets - first_row)[:, None] == column
        dlogits = jnp.where(hit_all, cotangent[:, None], 0.0)
        dlogits = (dlogits - scale[:, None] * raised.astype(f32)).astype(bf16)
        grad = jnp.dot(dlogits, head_weight, preferred_element_type=f32)
        grad = (grad * up).astype(f16)
        outer = (((0,), (0,)), ((), ()))
        weight_grad = lax.dot_general(dlogits, hidden, outer, preferred_element_type=f32)
        weight_grad = weight_grad.astype(bf16)

    with jax.named_scope("scatter_hidden_grad"):
        grad = turn(grad.reshape(sz["x"], -1, width), "x")
        grad = jnp.sum(grad.astype(f32), axis=0).astype(f16)
        grad = turn(grad.reshape(sz["z"], -1, width), "z")
        hidden_grad = (jnp.sum(grad.astype(f32), axis=0) * down).astype(bf16)

    with jax.named_scope("rewards"):
        next_value = jnp.concatenate([lse[1:], jnp.zeros((1,), f32)])
        rewards = picked - keep * next_value
    return (rewards, hidden_grad, weight_grad)


def solution(mesh):
    fine = Mesh(mesh.devices.reshape(4, 16, 4, 2), ("x", "z", "y", "c"))
    block = P(("x", "z"), ("y", "c"))
    return jax.shard_map(
        shards,
        mesh=fine,
        in_specs=(block, block, P(), P(), P()),
        out_specs=(P(), block, block),
        check_vma=False,
    )
```

```python
import jax
import jax.numpy as jnp
from jax import lax
from jax.sharding import Mesh, PartitionSpec as P

discount = 0.99
raise_logits = 8.0
raise_grad = 65536.0
f32 = jnp.float32
bf16 = jnp.bfloat16
f16 = jnp.float16


def spread(block, axis):
    copies = jnp.broadcast_to(block, (lax.axis_size(axis), *block.shape))
    copies = lax.all_to_all(copies, axis, 0, 0, tiled=True)
    return copies.reshape(-1, block.shape[-1])


def shards(hidden_states, head_weight, targets, terminal, cotangent):
    rows, width = head_weight.shape
    tokens = targets.shape[0]
    sz = {a: lax.axis_size(a) for a in ("x", "z", "y", "c")}
    n_width = sz["y"] * sz["c"]
    n_vocab = sz["x"] * sz["z"]
    own = tokens // n_width
    half = tokens // sz["c"]
    x, z, y, c = (lax.axis_index(a) for a in ("x", "z", "y", "c"))
    first_row = (x * sz["z"] + z) * rows
    first_token = (c * sz["y"] + y) * own
    is_low = c == 0
    swap = lambda v: lax.ppermute(v, "c", [(0, 1), (1, 0)])
    turn = lambda v, axis: lax.all_to_all(v, axis, 0, 0, tiled=True)
    cut = lambda v: lax.dynamic_slice(v, (first_token,), (own,))

    keep = discount * (1.0 - terminal.astype(f32))
    carried = jnp.concatenate([jnp.zeros((1,), f32), (keep * cotangent)[:-1]])
    unit = jnp.maximum(jnp.max(jnp.abs(cotangent)), 1e-30)
    down, up = lax.optimization_barrier((unit / raise_grad, raise_grad / unit))
    column = jnp.arange(rows, dtype=jnp.int32)

    with jax.named_scope("gather_hidden"):
        hidden = lax.all_gather(spread(hidden_states, "z"), "x", axis=0, tiled=True)

    with jax.named_scope("logits"):
        near_h = lax.dynamic_slice_in_dim(hidden, c * half, half)
        far_h = lax.dynamic_slice_in_dim(hidden, (1 - c) * half, half)
        inner = (((1,), (1,)), ((), ()))
        far_l = lax.dot_general(far_h, head_weight, inner, preferred_element_type=f32)
        far_l = swap((far_l * raise_logits).astype(f16))
        near_l = lax.dot_general(near_h, head_weight, inner, preferred_element_type=f32)
        near_l = lax.optimization_barrier(near_l)
        chip_l = (near_l * raise_logits + far_l.astype(f32)).astype(f16)
        pieces = turn(chip_l.reshape(sz["y"], own, rows), "y")
        logits = jnp.sum(pieces.astype(f32), axis=0) * (1.0 / raise_logits)

    with jax.named_scope("own_statistics"):
        hit = (cut(targets) - first_row)[:, None] == column
        own_top = jnp.max(logits, axis=1)
        raised = jnp.exp(logits - own_top[:, None])
        picked = jnp.sum(jnp.where(hit, logits, 0.0), axis=1)
        mine = jnp.concatenate([own_top + jnp.log(jnp.sum(raised, axis=1)), picked])
        mine = jnp.broadcast_to(mine, (n_vocab, 2 * own))

    with jax.named_scope("gather_raised"):
        near = lax.all_gather(raised.astype(bf16), "y", axis=0, tiled=True)
        far = swap(near)
        raised = jnp.concatenate([jnp.where(is_low, near, far), jnp.where(is_low, far, near)])

    with jax.named_scope("statistics"):
        every = turn(mine, ("z", "x"))
        top = jnp.max(every[:, :own], axis=0)
        lse = top + jnp.log(jnp.sum(jnp.exp(every[:, :own] - top), axis=0))
        picked = jnp.sum(every[:, own:], axis=0)
        parts = jnp.concatenate([lse, picked, cut(carried) * jnp.exp(own_top - lse), lse])
        parts, _ = lax.optimization_barrier((parts, near))
        parts = turn(jnp.broadcast_to(parts, (n_width, 4 * own)), ("c", "y"))
        lse, picked, scale, _ = (
            parts[:, i * own : (i + 1) * own].reshape(tokens) for i in range(4)
        )

    with jax.named_scope("products"):
        hit_all = (targets - first_row)[:, None] == column
        dlogits = jnp.where(hit_all, cotangent[:, None], 0.0)
        dlogits = (dlogits - scale[:, None] * raised.astype(f32)).astype(bf16)
        grad = jnp.dot(dlogits, head_weight, preferred_element_type=f32)
        grad = (grad * up).astype(f16)
        outer = (((0,), (0,)), ((), ()))
        weight_grad = lax.dot_general(dlogits, hidden, outer, preferred_element_type=f32)
        weight_grad = weight_grad.astype(bf16)

    with jax.named_scope("scatter_hidden_grad"):
        grad = turn(grad.reshape(sz["x"], -1, width), "x")
        grad = jnp.sum(grad.astype(f32), axis=0).astype(f16)
        grad = turn(grad.reshape(sz["z"], -1, width), "z")
        hidden_grad = (jnp.sum(grad.astype(f32), axis=0) * down).astype(bf16)

    with jax.named_scope("rewards"):
        next_value = jnp.concatenate([lse[1:], jnp.zeros((1,), f32)])
        rewards = picked - keep * next_value
    return (rewards, hidden_grad, weight_grad)


def solution(mesh):
    fine = Mesh(mesh.devices.reshape(4, 16, 4, 2), ("x", "z", "y", "c"))
    block = P(("x", "z"), ("y", "c"))
    return jax.shard_map(
        shards,
        mesh=fine,
        in_specs=(block, block, P(), P(), P()),
        out_specs=(P(), block, block),
        check_vma=False,
    )
```

```python
import jax
import jax.numpy as jnp
from jax import lax
from jax.sharding import Mesh, PartitionSpec as P

discount = 0.99
raise_logits = 8.0
raise_grad = 65536.0
f32 = jnp.float32
bf16 = jnp.bfloat16
f16 = jnp.float16


def spread(block, axis):
    copies = jnp.broadcast_to(block, (lax.axis_size(axis), *block.shape))
    copies = lax.all_to_all(copies, axis, 0, 0, tiled=True)
    return copies.reshape(-1, block.shape[-1])


def shards(hidden_states, head_weight, targets, terminal, cotangent):
    rows, width = head_weight.shape
    tokens = targets.shape[0]
    sz = {a: lax.axis_size(a) for a in ("x", "z", "y", "c")}
    n_width = sz["y"] * sz["c"]
    n_vocab = sz["x"] * sz["z"]
    own = tokens // n_width
    half = tokens // sz["c"]
    x, z, y, c = (lax.axis_index(a) for a in ("x", "z", "y", "c"))
    first_row = (x * sz["z"] + z) * rows
    first_token = (c * sz["y"] + y) * own
    is_low = c == 0
    swap = lambda v: lax.ppermute(v, "c", [(0, 1), (1, 0)])
    turn = lambda v, axis: lax.all_to_all(v, axis, 0, 0, tiled=True)
    cut = lambda v: lax.dynamic_slice(v, (first_token,), (own,))

    keep = discount * (1.0 - terminal.astype(f32))
    carried = jnp.concatenate([jnp.zeros((1,), f32), (keep * cotangent)[:-1]])
    unit = jnp.maximum(jnp.max(jnp.abs(cotangent)), 1e-30)
    down, up = lax.optimization_barrier((unit / raise_grad, raise_grad / unit))
    column = jnp.arange(rows, dtype=jnp.int32)

    with jax.named_scope("gather_hidden"):
        hidden = spread(spread(hidden_states, "z"), "x")

    with jax.named_scope("logits"):
        near_h = lax.dynamic_slice_in_dim(hidden, c * half, half)
        far_h = lax.dynamic_slice_in_dim(hidden, (1 - c) * half, half)
        inner = (((1,), (1,)), ((), ()))
        far_l = lax.dot_general(far_h, head_weight, inner, preferred_element_type=f32)
        far_l = swap((far_l * raise_logits).astype(f16))
        near_l = lax.dot_general(near_h, head_weight, inner, preferred_element_type=f32)
        near_l = lax.optimization_barrier(near_l)
        chip_l = (near_l * raise_logits + far_l.astype(f32)).astype(f16)
        pieces = turn(chip_l.reshape(sz["y"], own, rows), "y")
        logits = jnp.sum(pieces.astype(f32), axis=0) * (1.0 / raise_logits)

    with jax.named_scope("own_statistics"):
        hit = (cut(targets) - first_row)[:, None] == column
        own_top = jnp.max(logits, axis=1)
        raised = jnp.exp(logits - own_top[:, None])
        picked = jnp.sum(jnp.where(hit, logits, 0.0), axis=1)
        mine = jnp.concatenate([own_top + jnp.log(jnp.sum(raised, axis=1)), picked])
        mine = jnp.broadcast_to(mine, (n_vocab, 2 * own))

    with jax.named_scope("gather_raised"):
        near = lax.all_gather(raised.astype(bf16), "y", axis=0, tiled=True)
        far = swap(near)
        raised = jnp.concatenate([jnp.where(is_low, near, far), jnp.where(is_low, far, near)])
        raised = lax.optimization_barrier(raised)

    with jax.named_scope("statistics"):
        every = turn(mine, ("z", "x"))
        top = jnp.max(every[:, :own], axis=0)
        lse = top + jnp.log(jnp.sum(jnp.exp(every[:, :own] - top), axis=0))
        picked = jnp.sum(every[:, own:], axis=0)
        parts = jnp.concatenate([lse, picked, cut(carried) * jnp.exp(own_top - lse), lse])
        parts, _ = lax.optimization_barrier((parts, near))
        parts = turn(jnp.broadcast_to(parts, (n_width, 4 * own)), ("c", "y"))
        lse, picked, scale, _ = (
            parts[:, i * own : (i + 1) * own].reshape(tokens) for i in range(4)
        )

    with jax.named_scope("products"):
        hit_all = (targets - first_row)[:, None] == column
        dlogits = jnp.where(hit_all, cotangent[:, None], 0.0)
        dlogits = (dlogits - scale[:, None] * raised.astype(f32)).astype(bf16)
        grad = jnp.dot(dlogits, head_weight, preferred_element_type=f32)
        grad = (grad * up).astype(f16)
        outer = (((0,), (0,)), ((), ()))
        weight_grad = lax.dot_general(dlogits, hidden, outer, preferred_element_type=f32)
        weight_grad = weight_grad.astype(bf16)

    with jax.named_scope("scatter_hidden_grad"):
        grad = turn(grad.reshape(sz["x"], -1, width), "x")
        grad = jnp.sum(grad.astype(f32), axis=0).astype(f16)
        grad = turn(grad.reshape(sz["z"], -1, width), "z")
        hidden_grad = (jnp.sum(grad.astype(f32), axis=0) * down).astype(bf16)

    with jax.named_scope("rewards"):
        next_value = jnp.concatenate([lse[1:], jnp.zeros((1,), f32)])
        rewards = picked - keep * next_value
    return (rewards, hidden_grad, weight_grad)


def solution(mesh):
    fine = Mesh(mesh.devices.reshape(4, 16, 4, 2), ("x", "z", "y", "c"))
    block = P(("x", "z"), ("y", "c"))
    return jax.shard_map(
        shards,
        mesh=fine,
        in_specs=(block, block, P(), P(), P()),
        out_specs=(P(), block, block),
        check_vma=False,
    )
```

```python
import jax
import jax.numpy as jnp
from jax import lax
from jax.sharding import Mesh, PartitionSpec as P

discount = 0.99
raise_logits = 8.0
raise_grad = 65536.0
f32 = jnp.float32
bf16 = jnp.bfloat16
f16 = jnp.float16


def spread(block, axis):
    copies = jnp.broadcast_to(block, (lax.axis_size(axis), *block.shape))
    copies = lax.all_to_all(copies, axis, 0, 0, tiled=True)
    return copies.reshape(-1, block.shape[-1])


def shards(hidden_states, head_weight, targets, terminal, cotangent):
    rows, width = head_weight.shape
    tokens = targets.shape[0]
    sz = {a: lax.axis_size(a) for a in ("x", "z", "y", "c")}
    n_width = sz["y"] * sz["c"]
    n_vocab = sz["x"] * sz["z"]
    own = tokens // n_width
    half = tokens // sz["c"]
    x, z, y, c = (lax.axis_index(a) for a in ("x", "z", "y", "c"))
    first_row = (x * sz["z"] + z) * rows
    first_token = (c * sz["y"] + y) * own
    is_low = c == 0
    swap = lambda v: lax.ppermute(v, "c", [(0, 1), (1, 0)])
    turn = lambda v, axis: lax.all_to_all(v, axis, 0, 0, tiled=True)
    cut = lambda v: lax.dynamic_slice(v, (first_token,), (own,))

    keep = discount * (1.0 - terminal.astype(f32))
    carried = jnp.concatenate([jnp.zeros((1,), f32), (keep * cotangent)[:-1]])
    column = jnp.arange(rows, dtype=jnp.int32)

    with jax.named_scope("gather_hidden"):
        hidden = lax.all_gather(spread(hidden_states, "z"), "x", axis=0, tiled=True)

    hidden, held = lax.optimization_barrier((hidden, cotangent))
    unit = jnp.maximum(jnp.max(jnp.abs(held)), 1e-30)
    down, up = lax.optimization_barrier((unit / raise_grad, raise_grad / unit))

    with jax.named_scope("logits"):
        near_h = lax.dynamic_slice_in_dim(hidden, c * half, half)
        far_h = lax.dynamic_slice_in_dim(hidden, (1 - c) * half, half)
        inner = (((1,), (1,)), ((), ()))
        far_l = lax.dot_general(far_h, head_weight, inner, preferred_element_type=f32)
        far_l = swap((far_l * raise_logits).astype(f16))
        near_l = lax.dot_general(near_h, head_weight, inner, preferred_element_type=f32)
        near_l = lax.optimization_barrier(near_l)
        chip_l = (near_l * raise_logits + far_l.astype(f32)).astype(f16)
        pieces = turn(chip_l.reshape(sz["y"], own, rows), "y")
        logits = jnp.sum(pieces.astype(f32), axis=0) * (1.0 / raise_logits)

    with jax.named_scope("own_statistics"):
        hit = (cut(targets) - first_row)[:, None] == column
        own_top = jnp.max(logits, axis=1)
        raised = jnp.exp(logits - own_top[:, None])
        picked = jnp.sum(jnp.where(hit, logits, 0.0), axis=1)
        mine = jnp.concatenate([own_top + jnp.log(jnp.sum(raised, axis=1)), picked])
        mine = jnp.broadcast_to(mine, (n_vocab, 2 * own))

    with jax.named_scope("gather_raised"):
        near = lax.all_gather(raised.astype(bf16), "y", axis=0, tiled=True)
        far = swap(near)
        raised = jnp.concatenate([jnp.where(is_low, near, far), jnp.where(is_low, far, near)])

    with jax.named_scope("statistics"):
        every = turn(mine, ("z", "x"))
        top = jnp.max(every[:, :own], axis=0)
        lse = top + jnp.log(jnp.sum(jnp.exp(every[:, :own] - top), axis=0))
        picked = jnp.sum(every[:, own:], axis=0)
        parts = jnp.concatenate([lse, picked, cut(carried) * jnp.exp(own_top - lse), lse])
        parts, _ = lax.optimization_barrier((parts, near))
        parts = turn(jnp.broadcast_to(parts, (n_width, 4 * own)), ("c", "y"))
        lse, picked, scale, _ = (
            parts[:, i * own : (i + 1) * own].reshape(tokens) for i in range(4)
        )

    with jax.named_scope("products"):
        hit_all = (targets - first_row)[:, None] == column
        dlogits = jnp.where(hit_all, cotangent[:, None], 0.0)
        dlogits = (dlogits - scale[:, None] * raised.astype(f32)).astype(bf16)
        grad = jnp.dot(dlogits, head_weight, preferred_element_type=f32)
        grad = (grad * up).astype(f16)
        outer = (((0,), (0,)), ((), ()))
        weight_grad = lax.dot_general(dlogits, hidden, outer, preferred_element_type=f32)
        weight_grad = weight_grad.astype(bf16)

    with jax.named_scope("scatter_hidden_grad"):
        grad = turn(grad.reshape(sz["x"], -1, width), "x")
        grad = jnp.sum(grad.astype(f32), axis=0).astype(f16)
        grad = turn(grad.reshape(sz["z"], -1, width), "z")
        hidden_grad = (jnp.sum(grad.astype(f32), axis=0) * down).astype(bf16)

    with jax.named_scope("rewards"):
        next_value = jnp.concatenate([lse[1:], jnp.zeros((1,), f32)])
        rewards = picked - keep * next_value
    return (rewards, hidden_grad, weight_grad)


def solution(mesh):
    fine = Mesh(mesh.devices.reshape(4, 16, 4, 2), ("x", "z", "y", "c"))
    block = P(("x", "z"), ("y", "c"))
    return jax.shard_map(
        shards,
        mesh=fine,
        in_specs=(block, block, P(), P(), P()),
        out_specs=(P(), block, block),
        check_vma=False,
    )
```
